256 devices in a mesh: vox: 32 (over z, y), col: 8 (over x, core).
Axes of the slice: x: 4, y: 4, z: 8, core: 2. Of those that a mesh axis runs over, the one named last changes fastest.
Arguments:
- start_modes: float32 [128, 131072], P('col', 'vox'), may hold values from -48 to 48
- start_dirs: float32 [128, 131072], P('col', 'vox'), may hold values from -6 to 6
- coupling: float32 [13, 131072], P(None, ('vox', 'col')), may hold values from 0.05 to 1
- relax_class: int32 [131072], P(('vox', 'col')), may hold values from 0 to 3
- relaxivity: float32 [4], replicated, may hold values from 0.5 to 4
Outputs:
- modes: float32 [128, 131072], P('col', 'vox')
- ritz: float32 [128, 128], replicated
The draws below stay inside these ranges and needn't reach their ends.
All inputs are finite; a program needn't handle non-finite values.
Results may differ from the reference program's by a relative error of at most 0.0003.
Values sent between devices are 32-bit elements; how exact they have to be, the bound alone decides.
A program may use at most 64 MiB of HBM per device.

```python
import math
import jax
import jax.numpy as jnp
from jax import lax

K = 128
NX = 256
NZ = 2
HALF = 13
NCLASS = 4
ITERS = 2
QSTEPS = 3
NY = 256
NVOX = 131072


def draw_start_modes(key, part):
    base = jnp.clip(jax.random.normal(key, (K, NVOX), jnp.float32), -5.0, 5.0)
    plane = jnp.arange(NVOX, dtype=jnp.int32) // (NZ * NX)
    target = jnp.arange(K, dtype=jnp.int32) * NY // K
    heavy = plane[None, :] == target[:, None]
    return base * jnp.where(heavy, jnp.float32(8.0), jnp.float32(1.0))


def set_ends(entries, stream_key, smallest, top_value):
    place = [jax.random.randint(jax.random.fold_in(stream_key, axis), (), 0, length) for axis, length in enumerate(entries.shape)]
    main_axis = entries.shape.index(max(entries.shape))
    beside = place[:main_axis] + [(place[main_axis] + 1) % entries.shape[main_axis]] + place[main_axis + 1:]
    return entries.at[tuple(place)].set(smallest).at[tuple(beside)].set(top_value)


def block_levels(rng, dims, split, least, high):
    level = 1.0
    for axis_at, parts in split:
        draws = jax.random.uniform(jax.random.fold_in(jax.random.fold_in(rng, 6), axis_at), (parts,), jnp.float32, least / len(split), high / len(split))
        level = level * jnp.repeat(jnp.exp(draws), dims[axis_at] // parts).reshape((-1,) + (1,) * (len(dims) - 1 - axis_at))
    return level


def normal_values(rng, extent, deviation, most, split=(), held_as=jnp.bfloat16):
    factor_of = block_levels(rng, extent, split, -0.22, 0.18) if split else 1.0
    drawn = jax.random.normal(rng, extent, jnp.float32) * deviation * factor_of
    return jnp.minimum(jnp.maximum(drawn, -most), most).astype(held_as)


def setup_inputs(seed: int = 0) -> dict:
    seeds = jax.random.split(jax.random.key(seed), 6)
    return {
        "start_modes": draw_start_modes(jax.random.fold_in(seeds[5], 71), 0),
        "start_dirs": normal_values(seeds[1], (K, NVOX), 1.0, 6.0, ((0, 8), (1, 32)), jnp.float32),
        "coupling": jnp.clip(jnp.exp(math.log(1.0) - 2.9957323 * jax.random.uniform(seeds[2], (HALF, NVOX), jnp.float32) ** block_levels(seeds[2], (HALF, NVOX), ((1, 256),), -0.2, 0.2)), 0.05, 1.0),
        "relax_class": set_ends(jax.random.randint(seeds[3], (NVOX,), 0, NCLASS), jax.random.fold_in(seeds[3], 1), 0, NCLASS - 1).astype(jnp.int32),
        "relaxivity": jnp.clip(jnp.exp(jax.random.uniform(seeds[4], (NCLASS,), jnp.float32, math.log(0.5), math.log(4.0))), 0.5, 4.0),
    }


offsets = [(a, b, c) for a in (-1, 0, 1) for b in (-1, 0, 1) for c in (-1, 0, 1) if (a, b, c) > (0, 0, 0)]

def matmul(left, right):
    return jnp.dot(left.astype(jnp.float32), right.astype(jnp.float32), precision=lax.Precision.HIGHEST, preferred_element_type=jnp.float32)

def lower_solve(lower, rhs):
    return lax.linalg.triangular_solve(lower, rhs, left_side=True, lower=True)

def upper_solve(lower, rhs):
    return lax.linalg.triangular_solve(lower, rhs, left_side=True, lower=True, transpose_a=True)

def symmetric(matrix):
    return 0.5 * (matrix + matrix.T)

def project_pencil(gram_a, gram_b, count):
    sym_a = symmetric(gram_a)
    scales = lax.rsqrt(jnp.diagonal(gram_b) + 1e-06)
    normed_b = scales[:, None] * gram_b * scales[None, :]
    normed_a = scales[:, None] * sym_a * scales[None, :]
    lower = jnp.linalg.cholesky(normed_b)
    half_way = lower_solve(lower, normed_a)
    reduced = lower_solve(lower, half_way.T)
    shift = 2.0 * jnp.max(lax.optimization_barrier(jnp.sum(jnp.abs(reduced), axis=1)))
    iterate = jnp.eye(gram_a.shape[0], count, dtype=jnp.float32)
    for sweep_index in range(QSTEPS):
        iterate = shift * iterate - matmul(reduced, iterate)
        factor = jnp.linalg.cholesky(matmul(iterate.T, iterate))
        iterate = lower_solve(factor, iterate.T).T
    return scales[:, None] * upper_solve(lower, iterate)

def neighbour_sum(padded, coupled):
    rows_y = padded.shape[1] - 2
    rows_z = padded.shape[2] - 2
    rows_x = padded.shape[3] - 2
    total = jnp.zeros((padded.shape[0], rows_y, rows_z, rows_x), jnp.float32)
    for which, (step_y, step_z, step_x) in enumerate(offsets):
        ahead = padded[:, 1 + step_y:1 + step_y + rows_y, 1 + step_z:1 + step_z + rows_z, 1 + step_x:1 + step_x + rows_x]
        behind = padded[:, 1 - step_y:1 - step_y + rows_y, 1 - step_z:1 - step_z + rows_z, 1 - step_x:1 - step_x + rows_x]
        here = coupled[which, 1:1 + rows_y, 1:1 + rows_z, 1:1 + rows_x]
        back = coupled[which, 1 - step_y:1 - step_y + rows_y, 1 - step_z:1 - step_z + rows_z, 1 - step_x:1 - step_x + rows_x]
        total = total + here[None] * ahead
        total = total + back[None] * behind
    return total

def pad_grid(array):
    return jnp.pad(array, ((0, 0), (1, 1), (1, 1), (1, 1)))

def reference(start_modes, start_dirs, coupling, relax_class, relaxivity):
    match = relax_class[:, None] == jnp.arange(NCLASS, dtype=jnp.int32)[None, :]
    voxel_rate = lax.optimization_barrier(jnp.sum(jnp.where(match, relaxivity[None, :], jnp.float32(0.0)), axis=1))
    damping = 1.0 / (1.0 + voxel_rate)
    coupled = pad_grid(coupling.reshape(HALF, NY, NZ, NX))
    unity = pad_grid(jnp.ones((1, NY, NZ, NX), jnp.float32))
    degree = neighbour_sum(unity, coupled).reshape(NVOX)
    diagonal = degree + voxel_rate

    def operate(field):
        count = field.shape[0]
        padded = pad_grid(field.reshape(count, NY, NZ, NX))
        return diagonal[None, :] * field - neighbour_sum(padded, coupled).reshape(count, NVOX)
    modes = start_modes
    dirs = start_dirs
    images = operate(modes)
    dir_images = operate(dirs)
    ritz = symmetric(matmul(modes, images.T))
    for iteration in range(ITERS):
        resid = images - matmul(ritz, modes)
        search = resid * damping[None, :]
        search_images = operate(search)
        basis = jnp.concatenate([modes, search, dirs], axis=0)
        basis_images = jnp.concatenate([images, search_images, dir_images], axis=0)
        gram_a = matmul(basis, basis_images.T)
        gram_b = matmul(basis, basis.T)
        coeffs = project_pencil(gram_a, gram_b, K)
        modes = matmul(coeffs.T, basis)
        images = matmul(coeffs.T, basis_images)
        dirs = matmul(coeffs[K:].T, basis[K:])
        dir_images = matmul(coeffs[K:].T, basis_images[K:])
        ritz = symmetric(matmul(modes, images.T))
    return (modes * math.sqrt(NVOX), ritz)
```

```python
import functools
import math

import jax
import jax.numpy as jnp
from jax import lax
from jax.experimental import pallas as pl
from jax.experimental.pallas import tpu as pltpu
from jax.sharding import PartitionSpec as P

NX = 256
NZ = 2
HALF = 13
ITERS = 2
QSTEPS = 3


SIZES = {"core": 2, "x": 4, "y": 4, "z": 8}


def digit(axis):
    if axis in ("core", "x"):
        c = lax.axis_index("col")
        return lax.rem(c, 2) if axis == "core" else lax.div(c, 2)
    v = lax.axis_index("vox")
    return lax.rem(v, 4) if axis == "y" else lax.div(v, 4)


def peer(axis, step):
    size = SIZES[axis]
    other = lax.rem(digit(axis) + step, size)
    if axis == "core":
        return {"col": digit("x") * 2 + other}
    if axis == "x":
        return {"col": other * 2 + digit("core")}
    if axis == "y":
        return {"vox": digit("z") * 4 + other}
    return {"vox": other * 4 + digit("y")}


def greet(axes):
    barrier = pltpu.get_barrier_semaphore()
    count = 0
    for axis in axes:
        for step in range(1, SIZES[axis]):
            pl.semaphore_signal(barrier, inc=1, device_id=peer(axis, step), device_id_type=pl.DeviceIdType.MESH)
            count += 1
    pl.semaphore_wait(barrier, count)


class Part:
    def __init__(self, start, rows, stages):
        self.start, self.rows, self.stages = start, rows, stages

    def plan(self, scratch):
        self.steps = []
        rows = self.rows
        for axis, kind in self.stages:
            size = SIZES[axis]
            if kind == "scatter":
                rows = rows // size
            land = len(scratch)
            scratch.append(pltpu.VMEM((size, rows, 128), jnp.float32))
            held = len(scratch)
            scratch.append(pltpu.VMEM((rows, 128), jnp.float32))
            self.steps.append((axis, kind, rows, land, held))
        self.gathers = [s for s in self.steps if s[1] == "scatter"][::-1]


def sum_kernel(parts, axes, ncopies, in_ref, out_ref, *scratch):
    send, recv = scratch[-2], scratch[-1]
    greet(axes)
    copies = []

    def launch(src, dst, axis, step):
        k = len(copies)
        copy = pltpu.make_async_remote_copy(src_ref=src, dst_ref=dst, send_sem=send.at[k], recv_sem=recv.at[k],
                                            device_id=peer(axis, step), device_id_type=pl.DeviceIdType.MESH)
        copy.start()
        copies.append(copy)
        return copy

    state = []
    for part in parts:
        state.append({"ref": in_ref, "at": part.start, "start": part.start, "rows": part.rows, "waiting": None})

    def begin(part, st, s):
        if s < len(part.steps):
            axis, kind, rows, land, held = part.steps[s]
            size = SIZES[axis]
            me = digit(axis)
            waiting = []
            for step in range(1, size):
                if kind == "scatter":
                    other = lax.rem(me + step, size)
                    src = st["ref"].at[pl.ds(pl.multiple_of(st["at"] + other * rows, 8), rows)]
                else:
                    src = st["ref"].at[pl.ds(pl.multiple_of(st["at"], 8), rows)]
                waiting.append(launch(src, scratch[land].at[step], axis, step))
            st["waiting"] = waiting
        else:
            g = s - len(part.steps)
            axis, kind, rows, land, held = part.gathers[g]
            mine = out_ref.at[pl.ds(pl.multiple_of(st["start"], 8), rows)]
            st["waiting"] = [launch(mine, mine, axis, step) for step in range(1, SIZES[axis])]

    def finish(part, st, s):
        if s < len(part.steps):
            axis, kind, rows, land, held = part.steps[s]
            size = SIZES[axis]
            me = digit(axis)
            landing = scratch[land]
            for copy in st["waiting"]:
                copy.wait_recv()
            if kind == "scatter":
                at = pl.multiple_of(st["at"] + me * rows, 8)
                total = st["ref"][pl.ds(at, rows)]
                for step in range(1, size):
                    total = total + landing[step]
                st["start"] = st["start"] + me * rows
            else:
                landing[0] = st["ref"][pl.ds(pl.multiple_of(st["at"], 8), rows)]
                total = landing[me]
                for k in range(1, size):
                    total = total + landing[lax.rem(me - k + size, size)]
            if s == len(part.steps) - 1:
                out_ref[pl.ds(pl.multiple_of(st["start"], 8), rows)] = total
            else:
                scratch[held][...] = total
                st["ref"], st["at"] = scratch[held], 0
        else:
            axis, kind, rows, land, held = part.gathers[s - len(part.steps)]
            for copy in st["waiting"]:
                copy.wait_recv()
            st["start"] = st["start"] - digit(axis) * rows

    lengths = [len(p.steps) + len(p.gathers) for p in parts]
    for part, st in zip(parts, state):
        begin(part, st, 0)
    for s in range(max(lengths)):
        for part, st, n in zip(parts, state, lengths):
            if s < n:
                finish(part, st, s)
                if s + 1 < n:
                    begin(part, st, s + 1)
    for copy in copies:
        copy.wait_send()


def all_sum(array, layout, collective_id, name):
    parts = [Part(*p) for p in layout]
    scratch = []
    for p in parts:
        p.plan(scratch)
    axes = []
    ncopies = 0
    for p in parts:
        for axis, kind, *_ in p.steps:
            if axis not in axes:
                axes.append(axis)
            ncopies += (SIZES[axis] - 1) * (2 if kind == "scatter" else 1)
    scratch += [pltpu.SemaphoreType.DMA((ncopies,)), pltpu.SemaphoreType.DMA((ncopies,))]
    return pl.pallas_call(
        functools.partial(sum_kernel, parts, axes, ncopies),
        out_shape=jax.ShapeDtypeStruct(array.shape, jnp.float32),
        in_specs=[pl.BlockSpec(memory_space=pltpu.VMEM)],
        out_specs=pl.BlockSpec(memory_space=pltpu.VMEM),
        scratch_shapes=scratch,
        compiler_params=pltpu.CompilerParams(collective_id=collective_id, has_side_effects=True,
                                             vmem_limit_bytes=32 << 20),
        name=name,
    )(array)

RITZ_LAYOUT = [(0, 128, [("z", "scatter"), ("core", "exchange"), ("x", "exchange"), ("y", "exchange")])]
GRAM_LAYOUT = [
    (0, 768, [("core", "scatter"), ("x", "scatter"), ("y", "scatter"), ("z", "exchange")]),
    (768, 768, [("core", "scatter"), ("y", "scatter"), ("x", "scatter"), ("z", "exchange")]),
]


offsets = [
    (a, b, c) for a in (-1, 0, 1) for b in (-1, 0, 1) for c in (-1, 0, 1) if (a, b, c) > (0, 0, 0)
]


def from_behind(block, axis, distance):
    devices = range(lax.axis_size(axis))
    route = [(i - distance, i) for i in devices if i - distance in devices]
    return lax.ppermute(block, axis, route)


def extended_2(block, sides, width):
    for axis, dim in sides:
        count = lax.axis_size(axis)
        forward = [(i, i + 1) for i in range(count - 1)]
        backward = [(target, source) for source, target in forward]
        low = lax.ppermute(
            lax.slice_in_dim(block, block.shape[dim] - width, None, axis=dim), axis, forward
        )
        high = lax.ppermute(lax.slice_in_dim(block, 0, width, axis=dim), axis, backward)
        block = jnp.concatenate([low, block, high], axis=dim)
    return block


def matmul(left, right):
    return jnp.dot(left, right, precision=lax.Precision.HIGHEST, preferred_element_type=jnp.float32)


def lower_solve(lower, rhs):
    return lax.linalg.triangular_solve(lower, rhs, left_side=True, lower=True)


def upper_solve(lower, rhs):
    return lax.linalg.triangular_solve(lower, rhs, left_side=True, lower=True, transpose_a=True)


def symmetric(matrix):
    return 0.5 * (matrix + matrix.T)


def project_pencil(gram_a, gram_b, count):
    sym_a = symmetric(gram_a)
    scales = lax.rsqrt(jnp.diagonal(gram_b) + 1e-06)
    normed_b = scales[:, None] * gram_b * scales[None, :]
    normed_a = scales[:, None] * sym_a * scales[None, :]
    lower = jnp.linalg.cholesky(normed_b)
    half_way = lower_solve(lower, normed_a)
    reduced = lower_solve(lower, half_way.T)
    shift = 2.0 * jnp.max(jnp.sum(jnp.abs(reduced), axis=1))
    iterate = jnp.eye(gram_a.shape[0], count, dtype=jnp.float32)
    for sweep_index in range(QSTEPS):
        iterate = iterate - matmul(reduced, iterate) / shift
    factor = jnp.linalg.cholesky(matmul(iterate.T, iterate))
    iterate = lower_solve(factor, iterate.T).T
    coeffs = scales[:, None] * upper_solve(lower, iterate)
    return coeffs, symmetric(matmul(coeffs.T, matmul(sym_a, coeffs)))


def neighbour_sum(padded, coupled):
    rows_y = padded.shape[1] - 2
    rows_z = padded.shape[2] - 2
    rows_x = padded.shape[3] - 2
    total = jnp.zeros((padded.shape[0], rows_y, rows_z, rows_x), jnp.float32)
    for which, (step_y, step_z, step_x) in enumerate(offsets):
        ahead = padded[
            :,
            1 + step_y : 1 + step_y + rows_y,
            1 + step_z : 1 + step_z + rows_z,
            1 + step_x : 1 + step_x + rows_x,
        ]
        behind = padded[
            :,
            1 - step_y : 1 - step_y + rows_y,
            1 - step_z : 1 - step_z + rows_z,
            1 - step_x : 1 - step_x + rows_x,
        ]
        here = coupled[which, 1 : 1 + rows_y, 1 : 1 + rows_z, 1 : 1 + rows_x]
        back = coupled[
            which,
            1 - step_y : 1 - step_y + rows_y,
            1 - step_z : 1 - step_z + rows_z,
            1 - step_x : 1 - step_x + rows_x,
        ]
        total = total + here[None] * ahead
        total = total + back[None] * behind
    return total


def pad_plane(array):
    return jnp.pad(array, ((0, 0), (0, 0), (1, 1), (1, 1)))


def quotient(modes, images):
    return symmetric(all_sum(matmul(modes, images.T), RITZ_LAYOUT, 1, "ritz_sum"))


def gram_blocks(left, right):
    return [matmul(left[0], jnp.concatenate(right[:1]).T), matmul(left[1], jnp.concatenate(right[:2]).T),
            matmul(left[2], jnp.concatenate(right).T)]


def stacked(rows):
    return jnp.concatenate([row[:, 128 * k:128 * (k + 1)] for row in rows for k in range(row.shape[1] // 128)])


def unstacked(array):
    b = [array[128 * k:128 * (k + 1)] for k in range(6)]
    return jnp.block([[b[0], b[1].T, b[3].T], [b[1], b[2], b[4].T], [b[3], b[4], b[5]]])


def on_device(start_modes, start_dirs, coupling, relax_class, relaxivity):
    local_voxels = coupling.shape[1]
    match = relax_class[:, None] == jnp.arange(relaxivity.shape[0], dtype=jnp.int32)[None, :]
    voxel_rate = jnp.sum(jnp.where(match, relaxivity[None, :], jnp.float32(0.0)), axis=1)
    damping = 1.0 / (1.0 + voxel_rate)
    own_coupling = coupling.reshape(HALF, 1, NZ, NX)
    before = from_behind(own_coupling, ("vox", "col"), 1)
    coupled = pad_plane(
        jnp.concatenate([before, own_coupling, jnp.zeros_like(own_coupling)], axis=1)
    )
    position = lax.axis_index(("vox", "col"))
    device_count = lax.axis_size(("vox", "col"))
    plane = jnp.ones((1, 1, NZ, NX), jnp.float32)
    upper_flag = (position > 0).astype(jnp.float32)
    lower_flag = (position < device_count - 1).astype(jnp.float32)
    unity = pad_plane(jnp.concatenate([upper_flag * plane, plane, lower_flag * plane], axis=1))
    degree = neighbour_sum(unity, coupled).reshape(local_voxels)
    diagonal = degree + voxel_rate

    def operate(field):
        count = field.shape[0]
        shaped = field.reshape(count, 1, NZ, NX)
        extended = extended_2(shaped, ((("vox", "col"), 1),), 1)
        padded = pad_plane(extended)
        return diagonal[None, :] * field - neighbour_sum(padded, coupled).reshape(
            count, local_voxels
        )

    modes, dirs = (
        lax.all_to_all(start_modes, "col", split_axis=1, concat_axis=0, tiled=True),
        lax.all_to_all(start_dirs, "col", split_axis=1, concat_axis=0, tiled=True),
    )
    count = modes.shape[0]
    images = operate(modes)
    dir_images = operate(dirs)
    ritz = quotient(modes, images)
    for iteration in range(ITERS):
        resid = images - matmul(ritz, modes)
        search = resid * damping[None, :]
        search_images = operate(search)
        basis = jnp.concatenate([modes, search, dirs], axis=0)
        basis_images = jnp.concatenate([images, search_images, dir_images], axis=0)
        fields = [modes, search, dirs]
        local_a = stacked(gram_blocks(fields, [images, search_images, dir_images]))
        local_b = stacked(gram_blocks(fields, fields))
        summed = all_sum(jnp.concatenate([local_a, local_b]), GRAM_LAYOUT, 2, "gram_sum")
        coeffs, ritz = project_pencil(unstacked(summed[:768]), unstacked(summed[768:]), count)
        modes = matmul(coeffs.T, basis)
        images = matmul(coeffs.T, basis_images)
        dirs = matmul(coeffs[count:].T, basis[count:])
        dir_images = matmul(coeffs[count:].T, basis_images[count:])
    total_voxels = device_count * local_voxels
    scaled = modes * math.sqrt(total_voxels)
    modes_out = lax.all_to_all(scaled, "col", split_axis=0, concat_axis=1, tiled=True)
    return (modes_out, ritz)


def solution(mesh):
    in_specs = (P("col", "vox"), P("col", "vox"), P(None, ("vox", "col")), P(("vox", "col")), P())
    out_specs = (P("col", "vox"), P())
    return jax.shard_map(
        on_device, mesh=mesh, in_specs=in_specs, out_specs=out_specs, check_vma=False
    )
```

```python
import functools
import math

import jax
import jax.numpy as jnp
from jax import lax
from jax.experimental import pallas as pl
from jax.experimental.pallas import tpu as pltpu
from jax.sharding import PartitionSpec as P

NX = 256
NZ = 2
HALF = 13
ITERS = 2
QSTEPS = 3


SIZES = {"core": 2, "x": 4, "y": 4, "z": 8}


def digit(axis):
    if axis in ("core", "x"):
        c = lax.axis_index("col")
        return lax.rem(c, 2) if axis == "core" else lax.div(c, 2)
    v = lax.axis_index("vox")
    return lax.rem(v, 4) if axis == "y" else lax.div(v, 4)


def peer(axis, step):
    size = SIZES[axis]
    other = lax.rem(digit(axis) + step, size)
    if axis == "core":
        return {"col": digit("x") * 2 + other}
    if axis == "x":
        return {"col": other * 2 + digit("core")}
    if axis == "y":
        return {"vox": digit("z") * 4 + other}
    return {"vox": other * 4 + digit("y")}


def greet(axes):
    barrier = pltpu.get_barrier_semaphore()
    count = 0
    for axis in axes:
        for step in range(1, SIZES[axis]):
            pl.semaphore_signal(barrier, inc=1, device_id=peer(axis, step), device_id_type=pl.DeviceIdType.MESH)
            count += 1
    pl.semaphore_wait(barrier, count)


class Part:
    def __init__(self, start, rows, stages):
        self.start, self.rows, self.stages = start, rows, stages

    def plan(self, scratch):
        self.steps = []
        rows = self.rows
        for axis, kind in self.stages:
            size = SIZES[axis]
            if kind == "scatter":
                rows = rows // size
            land = len(scratch)
            scratch.append(pltpu.VMEM((size, rows, 128), jnp.float32))
            held = len(scratch)
            scratch.append(pltpu.VMEM((rows, 128), jnp.float32))
            self.steps.append((axis, kind, rows, land, held))
        self.gathers = [s for s in self.steps if s[1] == "scatter"][::-1]


def sum_kernel(parts, axes, ncopies, in_ref, out_ref, *scratch):
    send, recv = scratch[-2], scratch[-1]
    greet(axes)
    copies = []

    def launch(src, dst, axis, step):
        k = len(copies)
        copy = pltpu.make_async_remote_copy(src_ref=src, dst_ref=dst, send_sem=send.at[k], recv_sem=recv.at[k],
                                            device_id=peer(axis, step), device_id_type=pl.DeviceIdType.MESH)
        copy.start()
        copies.append(copy)
        return copy

    state = []
    for part in parts:
        state.append({"ref": in_ref, "at": part.start, "start": part.start, "rows": part.rows, "waiting": None})

    def begin(part, st, s):
        if s < len(part.steps):
            axis, kind, rows, land, held = part.steps[s]
            size = SIZES[axis]
            me = digit(axis)
            waiting = []
            for step in range(1, size):
                if kind == "scatter":
                    other = lax.rem(me + step, size)
                    src = st["ref"].at[pl.ds(pl.multiple_of(st["at"] + other * rows, 8), rows)]
                else:
                    src = st["ref"].at[pl.ds(pl.multiple_of(st["at"], 8), rows)]
                waiting.append(launch(src, scratch[land].at[step], axis, step))
            st["waiting"] = waiting
        else:
            g = s - len(part.steps)
            axis, kind, rows, land, held = part.gathers[g]
            mine = out_ref.at[pl.ds(pl.multiple_of(st["start"], 8), rows)]
            st["waiting"] = [launch(mine, mine, axis, step) for step in range(1, SIZES[axis])]

    def finish(part, st, s):
        if s < len(part.steps):
            axis, kind, rows, land, held = part.steps[s]
            size = SIZES[axis]
            me = digit(axis)
            landing = scratch[land]
            for copy in st["waiting"]:
                copy.wait_recv()
            if kind == "scatter":
                at = pl.multiple_of(st["at"] + me * rows, 8)
                total = st["ref"][pl.ds(at, rows)]
                for step in range(1, size):
                    total = total + landing[step]
                st["start"] = st["start"] + me * rows
            else:
                landing[0] = st["ref"][pl.ds(pl.multiple_of(st["at"], 8), rows)]
                total = landing[me]
                for k in range(1, size):
                    total = total + landing[lax.rem(me - k + size, size)]
            if s == len(part.steps) - 1:
                out_ref[pl.ds(pl.multiple_of(st["start"], 8), rows)] = total
            else:
                scratch[held][...] = total
                st["ref"], st["at"] = scratch[held], 0
        else:
            axis, kind, rows, land, held = part.gathers[s - len(part.steps)]
            for copy in st["waiting"]:
                copy.wait_recv()
            st["start"] = st["start"] - digit(axis) * rows

    lengths = [len(p.steps) + len(p.gathers) for p in parts]
    for part, st in zip(parts, state):
        begin(part, st, 0)
    for s in range(max(lengths)):
        for part, st, n in zip(parts, state, lengths):
            if s < n:
                finish(part, st, s)
                if s + 1 < n:
                    begin(part, st, s + 1)
    for copy in copies:
        copy.wait_send()


def all_sum(array, layout, collective_id, name):
    parts = [Part(*p) for p in layout]
    scratch = []
    for p in parts:
        p.plan(scratch)
    axes = []
    ncopies = 0
    for p in parts:
        for axis, kind, *_ in p.steps:
            if axis not in axes:
                axes.append(axis)
            ncopies += (SIZES[axis] - 1) * (2 if kind == "scatter" else 1)
    scratch += [pltpu.SemaphoreType.DMA((ncopies,)), pltpu.SemaphoreType.DMA((ncopies,))]
    return pl.pallas_call(
        functools.partial(sum_kernel, parts, axes, ncopies),
        out_shape=jax.ShapeDtypeStruct(array.shape, jnp.float32),
        in_specs=[pl.BlockSpec(memory_space=pltpu.VMEM)],
        out_specs=pl.BlockSpec(memory_space=pltpu.VMEM),
        scratch_shapes=scratch,
        compiler_params=pltpu.CompilerParams(collective_id=collective_id, has_side_effects=True,
                                             vmem_limit_bytes=32 << 20),
        name=name,
    )(array)

RITZ_LAYOUT = [(0, 128, [("z", "scatter"), ("core", "exchange"), ("x", "exchange"), ("y", "exchange")])]
GRAM_LAYOUT = [
    (0, 768, [("core", "scatter"), ("x", "scatter"), ("y", "scatter"), ("z", "exchange")]),
    (768, 768, [("core", "scatter"), ("y", "scatter"), ("x", "scatter"), ("z", "exchange")]),
]


offsets = [
    (a, b, c) for a in (-1, 0, 1) for b in (-1, 0, 1) for c in (-1, 0, 1) if (a, b, c) > (0, 0, 0)
]


def from_behind(block, axis, distance):
    devices = range(lax.axis_size(axis))
    route = [(i - distance, i) for i in devices if i - distance in devices]
    return lax.ppermute(block, axis, route)


def extended_2(block, sides, width):
    for axis, dim in sides:
        count = lax.axis_size(axis)
        forward = [(i, i + 1) for i in range(count - 1)]
        backward = [(target, source) for source, target in forward]
        low = lax.ppermute(
            lax.slice_in_dim(block, block.shape[dim] - width, None, axis=dim), axis, forward
        )
        high = lax.ppermute(lax.slice_in_dim(block, 0, width, axis=dim), axis, backward)
        block = jnp.concatenate([low, block, high], axis=dim)
    return block


def matmul(left, right):
    return jnp.dot(left, right, precision=lax.Precision.HIGHEST, preferred_element_type=jnp.float32)


def symmetric(matrix):
    return 0.5 * (matrix + matrix.T)


def product(left, right, over=(1, 0)):
    return lax.dot_general(
        left, right, (((over[0],), (over[1],)), ((), ())),
        precision=lax.Precision.HIGHEST, preferred_element_type=jnp.float32,
    )


SETTLED = 2e-3
MOST_STEPS = 10


def inverse_factor(matrix, step_ref, work_ref):
    n = matrix.shape[0]
    row = lax.broadcasted_iota(jnp.int32, (n, n), 0)
    col = lax.broadcasted_iota(jnp.int32, (n, n), 1)
    same = row == col
    unit = jnp.where(same, 1.0, 0.0)
    diag = jnp.where(same, matrix, 0.0)
    scale_row = lax.rsqrt(jnp.sum(diag, axis=0, keepdims=True))
    scale_col = lax.rsqrt(jnp.sum(diag, axis=1, keepdims=True))
    scaled = scale_col * matrix * scale_row

    def half(error):
        return jnp.where(row > col, error, jnp.where(same, 0.5 * error, 0.0))

    start = scaled - unit
    step_ref[...] = unit - half(start)

    def going(carry):
        count, size = carry
        return jnp.logical_and(count < MOST_STEPS, jnp.logical_not(size < SETTLED * SETTLED))

    def step(carry):
        count, _ = carry
        now = step_ref[...]
        error = product(product(now, scaled), now, (1, 1)) - unit
        step_ref[...] = now - product(half(error), now)
        return count + 1, jnp.sum(error * error)

    _, size = lax.while_loop(going, step, (jnp.int32(0), jnp.sum(start * start)))

    @pl.when(jnp.logical_not(size < SETTLED * SETTLED))
    def _():
        work_ref[...] = scaled
        step_ref[...] = unit

        def eliminate(j, carry):
            work, done = work_ref[...], step_ref[...]
            pivot_row = jnp.sum(jnp.where(row == j, work, 0.0), axis=0, keepdims=True)
            pivot_col = jnp.sum(jnp.where(col == j, work, 0.0), axis=1, keepdims=True)
            done_row = jnp.sum(jnp.where(row == j, done, 0.0), axis=0, keepdims=True)
            pivot = jnp.sum(jnp.where(same & (row == j), work, 0.0))
            factor = jnp.where(row > j, pivot_col / pivot, 0.0)
            work_ref[...] = work - factor * pivot_row
            done = done - factor * done_row
            step_ref[...] = jnp.where(row == j, done * lax.rsqrt(jnp.full((1, n), pivot)), done)
            return carry

        lax.fori_loop(0, n, eliminate, 0)

    return step_ref[...] * scale_row


def pencil_kernel(sum_ref, coeff_ref, ritz_ref, image_ref, inverse_ref, step_ref, work_ref):
    n = 128

    def block(k):
        return sum_ref[n * k:n * (k + 1)]

    row = lax.broadcasted_iota(jnp.int32, (n, n), 0)
    col = lax.broadcasted_iota(jnp.int32, (n, n), 1)
    same = row == col
    place = [(0, 0), (1, 0), (1, 1), (2, 0), (2, 1), (2, 2)]
    across, down = [], []
    for k in (6, 8, 11):
        diag = jnp.where(same, block(k), 0.0)
        across.append(lax.rsqrt(jnp.sum(diag, axis=0, keepdims=True) + 1e-06))
        down.append(lax.rsqrt(jnp.sum(diag, axis=1, keepdims=True) + 1e-06))
    normed = {}
    for k, (i, j) in enumerate(place):
        image = block(k)
        field = block(6 + k)
        if i == j:
            image = 0.5 * (image + image.T)
            field = 0.5 * (field + field.T)
        image_ref[n * i:n * (i + 1), n * j:n * (j + 1)] = image
        if i != j:
            image_ref[n * j:n * (j + 1), n * i:n * (i + 1)] = image.T
        normed[i, j] = down[i] * field * across[j]

    inverse_0 = inverse_factor(normed[0, 0], step_ref, work_ref)
    lower_10 = product(normed[1, 0], inverse_0, (1, 1))
    lower_20 = product(normed[2, 0], inverse_0, (1, 1))
    inverse_1 = inverse_factor(normed[1, 1] - product(lower_10, lower_10, (1, 1)), step_ref, work_ref)
    lower_21 = product(normed[2, 1] - product(lower_20, lower_10, (1, 1)), inverse_1, (1, 1))
    rest = normed[2, 2] - product(lower_20, lower_20, (1, 1)) - product(lower_21, lower_21, (1, 1))
    inverse_10 = -product(inverse_1, product(lower_10, inverse_0))
    inner_20 = product(lower_20, inverse_0) + product(lower_21, inverse_10)
    inner_21 = product(lower_21, inverse_1)
    inverse_2 = inverse_factor(rest, step_ref, work_ref)
    inverse_ref[...] = jnp.zeros((3 * n, 3 * n), jnp.float32)
    inverse_ref[0:n, 0:n] = inverse_0 * across[0]
    inverse_ref[n:2 * n, 0:n] = inverse_10 * across[0]
    inverse_ref[n:2 * n, n:2 * n] = inverse_1 * across[1]
    inverse_ref[2 * n:, 0:n] = -product(inverse_2, inner_20) * across[0]
    inverse_ref[2 * n:, n:2 * n] = -product(inverse_2, inner_21) * across[1]
    inverse_ref[2 * n:, 2 * n:] = inverse_2 * across[2]
    reduced = product(product(inverse_ref[...], image_ref[...]), inverse_ref[...], (1, 1))
    shift = 2.0 * jnp.max(jnp.sum(jnp.abs(reduced), axis=1, keepdims=True))
    reduced = reduced * (1.0 / jnp.full((1, 3 * n), shift))
    tall_row = lax.broadcasted_iota(jnp.int32, (3 * n, n), 0)
    tall_col = lax.broadcasted_iota(jnp.int32, (3 * n, n), 1)
    iterate = jnp.where(tall_row == tall_col, 1.0, 0.0) - reduced[:, :n]
    for _ in range(QSTEPS - 1):
        iterate = iterate - product(reduced, iterate)
    factor = inverse_factor(product(iterate, iterate, (0, 0)), step_ref, work_ref)
    iterate = product(iterate, factor, (1, 1))
    coeffs = product(inverse_ref[...], iterate, (0, 0))
    coeff_ref[...] = coeffs
    quotient = product(coeffs, product(image_ref[...], coeffs), (0, 0))
    ritz_ref[...] = 0.5 * (quotient + quotient.T)


def solve_pencil(summed):
    n = 128
    square = pltpu.VMEM((3 * n, 3 * n), jnp.float32)
    small = pltpu.VMEM((n, n), jnp.float32)
    return pl.pallas_call(
        pencil_kernel,
        out_shape=(jax.ShapeDtypeStruct((3 * n, n), jnp.float32), jax.ShapeDtypeStruct((n, n), jnp.float32)),
        in_specs=[pl.BlockSpec(memory_space=pltpu.VMEM)],
        out_specs=[pl.BlockSpec(memory_space=pltpu.VMEM)] * 2,
        scratch_shapes=[square, square, small, small],
        compiler_params=pltpu.CompilerParams(vmem_limit_bytes=32 << 20),
        name="pencil",
    )(summed)


def neighbour_sum(padded, coupled):
    rows_y = padded.shape[1] - 2
    rows_z = padded.shape[2] - 2
    rows_x = padded.shape[3] - 2
    total = jnp.zeros((padded.shape[0], rows_y, rows_z, rows_x), jnp.float32)
    for which, (step_y, step_z, step_x) in enumerate(offsets):
        ahead = padded[
            :,
            1 + step_y : 1 + step_y + rows_y,
            1 + step_z : 1 + step_z + rows_z,
            1 + step_x : 1 + step_x + rows_x,
        ]
        behind = padded[
            :,
            1 - step_y : 1 - step_y + rows_y,
            1 - step_z : 1 - step_z + rows_z,
            1 - step_x : 1 - step_x + rows_x,
        ]
        here = coupled[which, 1 : 1 + rows_y, 1 : 1 + rows_z, 1 : 1 + rows_x]
        back = coupled[
            which,
            1 - step_y : 1 - step_y + rows_y,
            1 - step_z : 1 - step_z + rows_z,
            1 - step_x : 1 - step_x + rows_x,
        ]
        total = total + here[None] * ahead
        total = total + back[None] * behind
    return total


def pad_plane(array):
    return jnp.pad(array, ((0, 0), (0, 0), (1, 1), (1, 1)))


def quotient(modes, images):
    return symmetric(all_sum(matmul(modes, images.T), RITZ_LAYOUT, 1, "ritz_sum"))


def gram_blocks(left, right):
    return [matmul(left[0], jnp.concatenate(right[:1]).T), matmul(left[1], jnp.concatenate(right[:2]).T),
            matmul(left[2], jnp.concatenate(right).T)]


def stacked(rows):
    return jnp.concatenate([row[:, 128 * k:128 * (k + 1)] for row in rows for k in range(row.shape[1] // 128)])


def on_device(start_modes, start_dirs, coupling, relax_class, relaxivity):
    local_voxels = coupling.shape[1]
    match = relax_class[:, None] == jnp.arange(relaxivity.shape[0], dtype=jnp.int32)[None, :]
    voxel_rate = jnp.sum(jnp.where(match, relaxivity[None, :], jnp.float32(0.0)), axis=1)
    damping = 1.0 / (1.0 + voxel_rate)
    own_coupling = coupling.reshape(HALF, 1, NZ, NX)
    before = from_behind(own_coupling, ("vox", "col"), 1)
    coupled = pad_plane(
        jnp.concatenate([before, own_coupling, jnp.zeros_like(own_coupling)], axis=1)
    )
    position = lax.axis_index(("vox", "col"))
    device_count = lax.axis_size(("vox", "col"))
    plane = jnp.ones((1, 1, NZ, NX), jnp.float32)
    upper_flag = (position > 0).astype(jnp.float32)
    lower_flag = (position < device_count - 1).astype(jnp.float32)
    unity = pad_plane(jnp.concatenate([upper_flag * plane, plane, lower_flag * plane], axis=1))
    degree = neighbour_sum(unity, coupled).reshape(local_voxels)
    diagonal = degree + voxel_rate

    def operate(field):
        count = field.shape[0]
        shaped = field.reshape(count, 1, NZ, NX)
        extended = extended_2(shaped, ((("vox", "col"), 1),), 1)
        padded = pad_plane(extended)
        return diagonal[None, :] * field - neighbour_sum(padded, coupled).reshape(
            count, local_voxels
        )

    modes, dirs = (
        lax.all_to_all(start_modes, "col", split_axis=1, concat_axis=0, tiled=True),
        lax.all_to_all(start_dirs, "col", split_axis=1, concat_axis=0, tiled=True),
    )
    count = modes.shape[0]
    images = operate(modes)
    dir_images = operate(dirs)
    ritz = quotient(modes, images)
    for iteration in range(ITERS):
        resid = images - matmul(ritz, modes)
        search = resid * damping[None, :]
        search_images = operate(search)
        basis = jnp.concatenate([modes, search, dirs], axis=0)
        basis_images = jnp.concatenate([images, search_images, dir_images], axis=0)
        fields = [modes, search, dirs]
        local_a = stacked(gram_blocks(fields, [images, search_images, dir_images]))
        local_b = stacked(gram_blocks(fields, fields))
        summed = all_sum(jnp.concatenate([local_a, local_b]), GRAM_LAYOUT, 2, "gram_sum")
        coeffs, ritz = solve_pencil(summed)
        modes = matmul(coeffs.T, basis)
        images = matmul(coeffs.T, basis_images)
        dirs = matmul(coeffs[count:].T, basis[count:])
        dir_images = matmul(coeffs[count:].T, basis_images[count:])
    total_voxels = device_count * local_voxels
    scaled = modes * math.sqrt(total_voxels)
    modes_out = lax.all_to_all(scaled, "col", split_axis=0, concat_axis=1, tiled=True)
    return (modes_out, ritz)


def solution(mesh):
    in_specs = (P("col", "vox"), P("col", "vox"), P(None, ("vox", "col")), P(("vox", "col")), P())
    out_specs = (P("col", "vox"), P())
    return jax.shard_map(
        on_device, mesh=mesh, in_specs=in_specs, out_specs=out_specs, check_vma=False
    )
```

```python
import functools
import math

import jax
import jax.numpy as jnp
from jax import lax
from jax.experimental import pallas as pl
from jax.experimental.pallas import tpu as pltpu
from jax.sharding import PartitionSpec as P

NX = 256
NZ = 2
HALF = 13
ITERS = 2
QSTEPS = 3


SIZES = {"core": 2, "x": 4, "y": 4, "z": 8}


def digit(axis):
    if axis in ("core", "x"):
        c = lax.axis_index("col")
        return lax.rem(c, 2) if axis == "core" else lax.div(c, 2)
    v = lax.axis_index("vox")
    return lax.rem(v, 4) if axis == "y" else lax.div(v, 4)


def peer(axis, step):
    size = SIZES[axis]
    other = lax.rem(digit(axis) + step, size)
    if axis == "core":
        return {"col": digit("x") * 2 + other}
    if axis == "x":
        return {"col": other * 2 + digit("core")}
    if axis == "y":
        return {"vox": digit("z") * 4 + other}
    return {"vox": other * 4 + digit("y")}


def beside(step):
    place = lax.rem(lax.axis_index("vox") * 8 + lax.axis_index("col") + step + 256, 256)
    return {"vox": lax.div(place, 8), "col": lax.rem(place, 8)}


def greet(axes):
    barrier = pltpu.get_barrier_semaphore()
    devices = [beside(1), beside(-1)]
    for axis in axes:
        devices += [peer(axis, step) for step in range(1, SIZES[axis])]
    for device in devices:
        pl.semaphore_signal(barrier, inc=1, device_id=device, device_id_type=pl.DeviceIdType.MESH)
    pl.semaphore_wait(barrier, len(devices))


class Copies:
    def __init__(self, send, recv):
        self.send, self.recv, self.all = send, recv, []

    def launch(self, src, dst, device):
        k = len(self.all)
        copy = pltpu.make_async_remote_copy(
            src_ref=src, dst_ref=dst, send_sem=self.send.at[k], recv_sem=self.recv.at[k],
            device_id=device, device_id_type=pl.DeviceIdType.MESH,
        )
        copy.start()
        self.all.append(copy)
        return copy

    def drain(self):
        for copy in self.all:
            copy.wait_send()


def plan(layout):
    rows, stages = layout
    scratch, steps, copies = [], [], 0
    for axis, kind in stages:
        size = SIZES[axis]
        if kind == "scatter":
            rows = rows // size
        scratch += [pltpu.VMEM((size, rows, 128), jnp.float32), pltpu.VMEM((rows, 128), jnp.float32)]
        steps.append((axis, kind, rows))
        copies += (size - 1) * (2 if kind == "scatter" else 1)
    return scratch, steps, copies


class Share:
    def __init__(self, layout, start, in_ref, out_ref, scratch, copies):
        _, self.steps, _ = plan(layout)
        self.gathers = [s for s in self.steps if s[1] == "scatter"][::-1]
        self.length = len(self.steps) + len(self.gathers)
        self.ref, self.at, self.start = in_ref, start, start
        self.out_ref, self.scratch, self.copies = out_ref, scratch, copies
        self.next = 0

    def begin(self):
        s = self.next
        self.waiting = []
        if s < len(self.steps):
            axis, kind, rows = self.steps[s]
            size = SIZES[axis]
            me = digit(axis)
            for step in range(1, size):
                if kind == "scatter":
                    at = self.at + lax.rem(me + step, size) * rows
                else:
                    at = self.at
                source = self.ref.at[pl.ds(pl.multiple_of(at, 8), rows)]
                self.waiting.append(self.copies.launch(source, self.scratch[2 * s].at[step], peer(axis, step)))
        elif s < self.length:
            axis, _, rows = self.gathers[s - len(self.steps)]
            mine = self.out_ref.at[pl.ds(pl.multiple_of(self.start, 8), rows)]
            self.waiting = [self.copies.launch(mine, mine, peer(axis, step)) for step in range(1, SIZES[axis])]

    def finish(self):
        s = self.next
        self.next += 1
        for copy in self.waiting:
            copy.wait_recv()
        if s < len(self.steps):
            axis, kind, rows = self.steps[s]
            size = SIZES[axis]
            me = digit(axis)
            landing = self.scratch[2 * s]
            if kind == "scatter":
                total = self.ref[pl.ds(pl.multiple_of(self.at + me * rows, 8), rows)]
                for step in range(1, size):
                    total = total + landing[step]
                self.start = self.start + me * rows
            else:
                landing[0] = self.ref[pl.ds(pl.multiple_of(self.at, 8), rows)]
                total = landing[me]
                for k in range(1, size):
                    total = total + landing[lax.rem(me - k + size, size)]
            if s == len(self.steps) - 1:
                self.out_ref[pl.ds(pl.multiple_of(self.start, 8), rows)] = total
            else:
                self.scratch[2 * s + 1][...] = total
                self.ref, self.at = self.scratch[2 * s + 1], 0
        elif s < self.length:
            axis, _, rows = self.gathers[s - len(self.steps)]
            self.start = self.start - digit(axis) * rows

    def turn(self):
        if self.next < self.length:
            self.finish()
            self.begin()


def through(shares):
    while any(s.next < s.length for s in shares):
        for share in shares:
            share.turn()


STRIP = 16


def apply_operator(field_ref, before_ref, after_ref, weight_ref, image_ref):
    width = field_ref.shape[1]

    def strip(k, carry):
        rows = pl.ds(pl.multiple_of(k * STRIP, STRIP), STRIP)
        sources = []
        for ref in (before_ref, field_ref, after_ref):
            value = ref[rows, :]
            sources.append(value)
            sources.append(jnp.concatenate([value[:, width // 2:], value[:, :width // 2]], axis=1))
        total = None
        for d, shift in enumerate((1, 0, width - 1)):
            part = weight_ref[6 * d:6 * d + 1, :] * sources[0]
            for m in range(1, 6):
                part = part + weight_ref[6 * d + m:6 * d + m + 1, :] * sources[m]
            if shift:
                part = pltpu.roll(part, shift, axis=1)
            total = part if total is None else total + part
        image_ref[rows, :] = total
        return carry

    lax.fori_loop(0, field_ref.shape[0] // STRIP, strip, 0)


def send_rows(copies, field_ref, before_ref, after_ref):
    return [copies.launch(field_ref, before_ref, beside(1)), copies.launch(field_ref, after_ref, beside(-1))]


RITZ_LAYOUT = (128, [("core", "scatter"), ("z", "scatter"), ("x", "exchange"), ("y", "exchange")])
GRAM_LAYOUTS = [
    (768, [("core", "scatter"), ("x", "scatter"), ("y", "scatter"), ("z", "exchange")]),
    (768, [("core", "scatter"), ("y", "scatter"), ("x", "scatter"), ("z", "exchange")]),
]
AXES = ("core", "x", "y", "z")


def start_kernel(modes_ref, dirs_ref, weight_ref, image_ref, dir_image_ref, ritz_ref, *scratch):
    before, after, dir_before, dir_after, local = scratch[:5]
    copies = Copies(*scratch[-2:])
    greet(AXES)
    halo = send_rows(copies, modes_ref, before, after)
    dir_halo = send_rows(copies, dirs_ref, dir_before, dir_after)
    for copy in halo:
        copy.wait_recv()
    apply_operator(modes_ref, before, after, weight_ref, image_ref)
    local[...] = product(modes_ref[...], image_ref[...], (1, 1))
    share = Share(RITZ_LAYOUT, 0, local, ritz_ref, scratch[5:-2], copies)
    share.begin()
    share.turn()
    for copy in dir_halo:
        copy.wait_recv()
    apply_operator(dirs_ref, dir_before, dir_after, weight_ref, dir_image_ref)
    through([share])
    copies.drain()


def search_kernel(modes_ref, images_ref, dirs_ref, dir_images_ref, ritz_ref, damping_ref, weight_ref,
                  search_ref, search_image_ref, sum_ref, *scratch):
    n = 128
    before, after, local = scratch[:3]
    rest = scratch[3:-2]
    half = len(rest) // 2
    copies = Copies(*scratch[-2:])
    greet(AXES)
    search = (images_ref[...] - product(ritz_ref[...], modes_ref[...])) * damping_ref[...]
    search_ref[...] = search
    halo = send_rows(copies, search_ref, before, after)

    def put(k, left_ref, right_ref):
        local[n * k:n * (k + 1)] = product(left_ref[...], right_ref[...], (1, 1))

    put(6, modes_ref, modes_ref)
    put(7, search_ref, modes_ref)
    put(8, search_ref, search_ref)
    put(9, dirs_ref, modes_ref)
    put(10, dirs_ref, search_ref)
    put(11, dirs_ref, dirs_ref)
    fields = Share(GRAM_LAYOUTS[0], 768, local, sum_ref, rest[:half], copies)
    fields.begin()
    put(0, modes_ref, images_ref)
    put(1, search_ref, images_ref)
    put(3, dirs_ref, images_ref)
    put(4, dir_images_ref, search_ref)
    put(5, dirs_ref, dir_images_ref)
    fields.turn()
    for copy in halo:
        copy.wait_recv()
    apply_operator(search_ref, before, after, weight_ref, search_image_ref)
    put(2, search_ref, search_image_ref)
    images = Share(GRAM_LAYOUTS[1], 0, local, sum_ref, rest[half:], copies)
    images.begin()
    through([fields, images])
    copies.drain()


def call_remote(kernel, name, collective_id, outs, landing, local_rows, layouts, operands, halos):
    scratch = [pltpu.VMEM((128, 512), jnp.float32)] * landing + [pltpu.VMEM((local_rows, 128), jnp.float32)]
    count = halos
    for layout in layouts:
        share_scratch, _, copies = plan(layout)
        scratch += share_scratch
        count += copies
    scratch += [pltpu.SemaphoreType.DMA((count,))] * 2
    vmem = pl.BlockSpec(memory_space=pltpu.VMEM)
    return pl.pallas_call(
        kernel,
        out_shape=tuple(jax.ShapeDtypeStruct(shape, jnp.float32) for shape in outs),
        in_specs=[vmem] * len(operands),
        out_specs=[vmem] * len(outs),
        scratch_shapes=scratch,
        compiler_params=pltpu.CompilerParams(
            collective_id=collective_id, has_side_effects=True, vmem_limit_bytes=32 << 20
        ),
        name=name,
    )(*operands)


offsets = [
    (a, b, c) for a in (-1, 0, 1) for b in (-1, 0, 1) for c in (-1, 0, 1) if (a, b, c) > (0, 0, 0)
]


def from_behind(block, axis, distance):
    devices = range(lax.axis_size(axis))
    route = [(i - distance, i) for i in devices if i - distance in devices]
    return lax.ppermute(block, axis, route)


def matmul(left, right):
    return jnp.dot(left, right, precision=lax.Precision.HIGHEST, preferred_element_type=jnp.float32)


def symmetric(matrix):
    return 0.5 * (matrix + matrix.T)


def product(left, right, over=(1, 0)):
    return lax.dot_general(
        left, right, (((over[0],), (over[1],)), ((), ())),
        precision=lax.Precision.HIGHEST, preferred_element_type=jnp.float32,
    )


SETTLED = 2e-3
MOST_STEPS = 10


def inverse_factor(matrix, step_ref, work_ref):
    n = matrix.shape[0]
    row = lax.broadcasted_iota(jnp.int32, (n, n), 0)
    col = lax.broadcasted_iota(jnp.int32, (n, n), 1)
    same = row == col
    unit = jnp.where(same, 1.0, 0.0)
    diag = jnp.where(same, matrix, 0.0)
    scale_row = lax.rsqrt(jnp.sum(diag, axis=0, keepdims=True))
    scale_col = lax.rsqrt(jnp.sum(diag, axis=1, keepdims=True))
    scaled = scale_col * matrix * scale_row

    def half(error):
        return jnp.where(row > col, error, jnp.where(same, 0.5 * error, 0.0))

    start = scaled - unit
    step_ref[...] = unit - half(start)

    def going(carry):
        count, size = carry
        return jnp.logical_and(count < MOST_STEPS, jnp.logical_not(size < SETTLED * SETTLED))

    def step(carry):
        count, _ = carry
        now = step_ref[...]
        error = product(product(now, scaled), now, (1, 1)) - unit
        step_ref[...] = now - product(half(error), now)
        return count + 1, jnp.sum(error * error)

    _, size = lax.while_loop(going, step, (jnp.int32(0), jnp.sum(start * start)))

    @pl.when(jnp.logical_not(size < SETTLED * SETTLED))
    def _():
        work_ref[...] = scaled
        step_ref[...] = unit

        def eliminate(j, carry):
            work, done = work_ref[...], step_ref[...]
            pivot_row = jnp.sum(jnp.where(row == j, work, 0.0), axis=0, keepdims=True)
            pivot_col = jnp.sum(jnp.where(col == j, work, 0.0), axis=1, keepdims=True)
            done_row = jnp.sum(jnp.where(row == j, done, 0.0), axis=0, keepdims=True)
            pivot = jnp.sum(jnp.where(same & (row == j), work, 0.0))
            factor = jnp.where(row > j, pivot_col / pivot, 0.0)
            work_ref[...] = work - factor * pivot_row
            done = done - factor * done_row
            step_ref[...] = jnp.where(row == j, done * lax.rsqrt(jnp.full((1, n), pivot)), done)
            return carry

        lax.fori_loop(0, n, eliminate, 0)

    return step_ref[...] * scale_row


def pencil_kernel(sum_ref, coeff_ref, ritz_ref, image_ref, inverse_ref, step_ref, work_ref):
    n = 128

    def block(k):
        return sum_ref[n * k:n * (k + 1)]

    row = lax.broadcasted_iota(jnp.int32, (n, n), 0)
    col = lax.broadcasted_iota(jnp.int32, (n, n), 1)
    same = row == col
    place = [(0, 0), (1, 0), (1, 1), (2, 0), (2, 1), (2, 2)]
    across, down = [], []
    for k in (6, 8, 11):
        diag = jnp.where(same, block(k), 0.0)
        across.append(lax.rsqrt(jnp.sum(diag, axis=0, keepdims=True) + 1e-06))
        down.append(lax.rsqrt(jnp.sum(diag, axis=1, keepdims=True) + 1e-06))
    normed = {}
    for k, (i, j) in enumerate(place):
        image = block(k)
        field = block(6 + k)
        if i == j:
            image = 0.5 * (image + image.T)
            field = 0.5 * (field + field.T)
        image_ref[n * i:n * (i + 1), n * j:n * (j + 1)] = image
        if i != j:
            image_ref[n * j:n * (j + 1), n * i:n * (i + 1)] = image.T
        normed[i, j] = down[i] * field * across[j]

    inverse_0 = inverse_factor(normed[0, 0], step_ref, work_ref)
    lower_10 = product(normed[1, 0], inverse_0, (1, 1))
    lower_20 = product(normed[2, 0], inverse_0, (1, 1))
    inverse_1 = inverse_factor(normed[1, 1] - product(lower_10, lower_10, (1, 1)), step_ref, work_ref)
    lower_21 = product(normed[2, 1] - product(lower_20, lower_10, (1, 1)), inverse_1, (1, 1))
    rest = normed[2, 2] - product(lower_20, lower_20, (1, 1)) - product(lower_21, lower_21, (1, 1))
    inverse_10 = -product(inverse_1, product(lower_10, inverse_0))
    inner_20 = product(lower_20, inverse_0) + product(lower_21, inverse_10)
    inner_21 = product(lower_21, inverse_1)
    inverse_2 = inverse_factor(rest, step_ref, work_ref)
    inverse_ref[...] = jnp.zeros((3 * n, 3 * n), jnp.float32)
    inverse_ref[0:n, 0:n] = inverse_0 * across[0]
    inverse_ref[n:2 * n, 0:n] = inverse_10 * across[0]
    inverse_ref[n:2 * n, n:2 * n] = inverse_1 * across[1]
    inverse_ref[2 * n:, 0:n] = -product(inverse_2, inner_20) * across[0]
    inverse_ref[2 * n:, n:2 * n] = -product(inverse_2, inner_21) * across[1]
    inverse_ref[2 * n:, 2 * n:] = inverse_2 * across[2]
    reduced = product(product(inverse_ref[...], image_ref[...]), inverse_ref[...], (1, 1))
    shift = 2.0 * jnp.max(jnp.sum(jnp.abs(reduced), axis=1, keepdims=True))
    reduced = reduced * (1.0 / jnp.full((1, 3 * n), shift))
    tall_row = lax.broadcasted_iota(jnp.int32, (3 * n, n), 0)
    tall_col = lax.broadcasted_iota(jnp.int32, (3 * n, n), 1)
    iterate = jnp.where(tall_row == tall_col, 1.0, 0.0) - reduced[:, :n]
    for _ in range(QSTEPS - 1):
        iterate = iterate - product(reduced, iterate)
    factor = inverse_factor(product(iterate, iterate, (0, 0)), step_ref, work_ref)
    iterate = product(iterate, factor, (1, 1))
    coeffs = product(inverse_ref[...], iterate, (0, 0))
    coeff_ref[...] = coeffs
    quotient = product(coeffs, product(image_ref[...], coeffs), (0, 0))
    ritz_ref[...] = 0.5 * (quotient + quotient.T)


def solve_pencil(summed):
    n = 128
    square = pltpu.VMEM((3 * n, 3 * n), jnp.float32)
    small = pltpu.VMEM((n, n), jnp.float32)
    return pl.pallas_call(
        pencil_kernel,
        out_shape=(jax.ShapeDtypeStruct((3 * n, n), jnp.float32), jax.ShapeDtypeStruct((n, n), jnp.float32)),
        in_specs=[pl.BlockSpec(memory_space=pltpu.VMEM)],
        out_specs=[pl.BlockSpec(memory_space=pltpu.VMEM)] * 2,
        scratch_shapes=[square, square, small, small],
        compiler_params=pltpu.CompilerParams(vmem_limit_bytes=32 << 20),
        name="pencil",
    )(summed)


def row_weights(own, before, first, last, rate):
    def inner(block, dz, dx):
        padded = jnp.pad(block, ((1, 1), (1, 1)))
        return padded[1 - dz:1 - dz + NZ, 1 - dx:1 - dx + NX]

    z = lax.broadcasted_iota(jnp.int32, (NZ, NX), 0)
    x = lax.broadcasted_iota(jnp.int32, (NZ, NX), 1)
    table = {}
    for which, (dy, dz, dx) in enumerate(offsets):
        inside = (z + dz >= 0) & (z + dz < NZ) & (x + dx >= 0) & (x + dx < NX)
        if dy:
            inside = inside & jnp.logical_not(last)
        table[dy, dz, dx] = jnp.where(inside, own[which], 0.0)
        if dy:
            table[-dy, -dz, -dx] = jnp.where(first, 0.0, inner(before[which], dz, dx))
        else:
            table[-dy, -dz, -dx] = inner(own[which], dz, dx)
    degree = sum(table.values())
    rows = []
    for dx in (-1, 0, 1):
        for dy in (-1, 0, 1):
            if (dy, dx) == (0, 0):
                same = degree + rate
            else:
                same = -table[dy, 0, dx]
            other = -(table[dy, 1, dx] + table[dy, -1, dx])
            rows += [jnp.roll(block.reshape(NZ * NX), dx) for block in (same, other)]
    return jnp.stack(rows)


def on_device(start_modes, start_dirs, coupling, relax_class, relaxivity):
    local_voxels = coupling.shape[1]
    match = relax_class[:, None] == jnp.arange(relaxivity.shape[0], dtype=jnp.int32)[None, :]
    voxel_rate = jnp.sum(jnp.where(match, relaxivity[None, :], jnp.float32(0.0)), axis=1)
    damping = 1.0 / (1.0 + voxel_rate)
    own = coupling.reshape(HALF, NZ, NX)
    before = from_behind(own, ("vox", "col"), 1)
    position = lax.axis_index(("vox", "col"))
    device_count = lax.axis_size(("vox", "col"))
    weights = row_weights(own, before, position == 0, position == device_count - 1, voxel_rate.reshape(NZ, NX))

    modes, dirs = (
        lax.all_to_all(start_modes, "col", split_axis=1, concat_axis=0, tiled=True),
        lax.all_to_all(start_dirs, "col", split_axis=1, concat_axis=0, tiled=True),
    )
    count = modes.shape[0]
    row, small = (count, local_voxels), (count, count)
    images, dir_images, ritz = call_remote(
        start_kernel, "start", 1, (row, row, small), 4, 128, [RITZ_LAYOUT], (modes, dirs, weights), 4
    )
    ritz = symmetric(ritz)
    for iteration in range(ITERS):
        search, search_images, summed = call_remote(
            search_kernel, "search", 2, (row, row, (12 * count, count)), 2, 12 * count, GRAM_LAYOUTS,
            (modes, images, dirs, dir_images, ritz, damping[None, :], weights), 2,
        )
        basis = jnp.concatenate([modes, search, dirs], axis=0)
        basis_images = jnp.concatenate([images, search_images, dir_images], axis=0)
        coeffs, ritz = solve_pencil(summed)
        modes = matmul(coeffs.T, basis)
        images = matmul(coeffs.T, basis_images)
        dirs = matmul(coeffs[count:].T, basis[count:])
        dir_images = matmul(coeffs[count:].T, basis_images[count:])
    total_voxels = device_count * local_voxels
    scaled = modes * math.sqrt(total_voxels)
    modes_out = lax.all_to_all(scaled, "col", split_axis=0, concat_axis=1, tiled=True)
    return (modes_out, ritz)


def solution(mesh):
    in_specs = (P("col", "vox"), P("col", "vox"), P(None, ("vox", "col")), P(("vox", "col")), P())
    out_specs = (P("col", "vox"), P())
    return jax.shard_map(
        on_device, mesh=mesh, in_specs=in_specs, out_specs=out_specs, check_vma=False
    )
```

```python
import functools
import math

import jax
import jax.numpy as jnp
from jax import lax
from jax.experimental import pallas as pl
from jax.experimental.pallas import tpu as pltpu
from jax.sharding import PartitionSpec as P

NX = 256
NZ = 2
HALF = 13
ITERS = 2
QSTEPS = 3


SIZES = {"core": 2, "x": 4, "y": 4, "z": 8}


def digit(axis):
    if axis in ("core", "x"):
        c = lax.axis_index("col")
        return lax.rem(c, 2) if axis == "core" else lax.div(c, 2)
    v = lax.axis_index("vox")
    return lax.rem(v, 4) if axis == "y" else lax.div(v, 4)


def peer(axis, step):
    size = SIZES[axis]
    other = lax.rem(digit(axis) + step, size)
    if axis == "core":
        return {"col": digit("x") * 2 + other}
    if axis == "x":
        return {"col": other * 2 + digit("core")}
    if axis == "y":
        return {"vox": digit("z") * 4 + other}
    return {"vox": other * 4 + digit("y")}


def beside(step):
    place = lax.rem(lax.axis_index("vox") * 8 + lax.axis_index("col") + step + 256, 256)
    return {"vox": lax.div(place, 8), "col": lax.rem(place, 8)}


def column(step):
    return {"col": lax.rem(lax.axis_index("col") + step, 8)}


def along(axes):
    return [peer(axis, step) for axis in axes for step in range(1, SIZES[axis])]


def hail(devices):
    barrier = pltpu.get_barrier_semaphore()
    for device in devices:
        pl.semaphore_signal(barrier, inc=1, device_id=device, device_id_type=pl.DeviceIdType.MESH)


def heard(devices):
    pl.semaphore_wait(pltpu.get_barrier_semaphore(), len(devices))


class Copies:
    def __init__(self, send, recv):
        self.send, self.recv, self.all = send, recv, []

    def launch(self, src, dst, device):
        k = len(self.all)
        copy = pltpu.make_async_remote_copy(
            src_ref=src, dst_ref=dst, send_sem=self.send.at[k], recv_sem=self.recv.at[k],
            device_id=device, device_id_type=pl.DeviceIdType.MESH,
        )
        copy.start()
        self.all.append(copy)
        return copy

    def drain(self):
        for copy in self.all:
            copy.wait_send()


def plan(layout):
    rows, stages = layout
    scratch, steps, copies = [], [], 0
    for axis, kind in stages:
        size = SIZES[axis]
        if kind == "scatter":
            rows = rows // size
        scratch += [pltpu.VMEM((size, rows, 128), jnp.float32), pltpu.VMEM((rows, 128), jnp.float32)]
        steps.append((axis, kind, rows))
        copies += (size - 1) * (2 if kind == "scatter" else 1)
    return scratch, steps, copies


class Share:
    def __init__(self, layout, start, in_ref, out_ref, scratch, copies):
        _, self.steps, _ = plan(layout)
        self.gathers = [s for s in self.steps if s[1] == "scatter"][::-1]
        self.length = len(self.steps) + len(self.gathers)
        self.ref, self.at, self.start = in_ref, start, start
        self.out_ref, self.scratch, self.copies = out_ref, scratch, copies
        self.next = 0

    def begin(self):
        s = self.next
        self.waiting = []
        if s < len(self.steps):
            axis, kind, rows = self.steps[s]
            size = SIZES[axis]
            me = digit(axis)
            for step in range(1, size):
                if kind == "scatter":
                    at = self.at + lax.rem(me + step, size) * rows
                else:
                    at = self.at
                source = self.ref.at[pl.ds(pl.multiple_of(at, 8), rows)]
                self.waiting.append(self.copies.launch(source, self.scratch[2 * s].at[step], peer(axis, step)))
        elif s < self.length:
            axis, _, rows = self.gathers[s - len(self.steps)]
            mine = self.out_ref.at[pl.ds(pl.multiple_of(self.start, 8), rows)]
            self.waiting = [self.copies.launch(mine, mine, peer(axis, step)) for step in range(1, SIZES[axis])]

    def finish(self):
        s = self.next
        self.next += 1
        for copy in self.waiting:
            copy.wait_recv()
        if s < len(self.steps):
            axis, kind, rows = self.steps[s]
            size = SIZES[axis]
            me = digit(axis)
            landing = self.scratch[2 * s]
            if kind == "scatter":
                total = self.ref[pl.ds(pl.multiple_of(self.at + me * rows, 8), rows)]
                for step in range(1, size):
                    total = total + landing[step]
                self.start = self.start + me * rows
            else:
                landing[0] = self.ref[pl.ds(pl.multiple_of(self.at, 8), rows)]
                total = landing[me]
                for k in range(1, size):
                    total = total + landing[lax.rem(me - k + size, size)]
            if s == len(self.steps) - 1:
                self.out_ref[pl.ds(pl.multiple_of(self.start, 8), rows)] = total
            else:
                self.scratch[2 * s + 1][...] = total
                self.ref, self.at = self.scratch[2 * s + 1], 0
        elif s < self.length:
            axis, _, rows = self.gathers[s - len(self.steps)]
            self.start = self.start - digit(axis) * rows

    def turn(self):
        if self.next < self.length:
            self.finish()
            self.begin()


def through(shares):
    while any(s.next < s.length for s in shares):
        for share in shares:
            share.turn()


STRIP = 16


def apply_operator(field_ref, before_ref, after_ref, weight_ref, image_ref):
    width = field_ref.shape[1]

    def strip(k, carry):
        rows = pl.ds(pl.multiple_of(k * STRIP, STRIP), STRIP)
        sources = []
        for ref in (before_ref, field_ref, after_ref):
            value = ref[rows, :]
            sources.append(value)
            sources.append(jnp.concatenate([value[:, width // 2:], value[:, :width // 2]], axis=1))
        total = None
        for d, shift in enumerate((1, 0, width - 1)):
            part = weight_ref[6 * d:6 * d + 1, :] * sources[0]
            for m in range(1, 6):
                part = part + weight_ref[6 * d + m:6 * d + m + 1, :] * sources[m]
            if shift:
                part = pltpu.roll(part, shift, axis=1)
            total = part if total is None else total + part
        image_ref[rows, :] = total
        return carry

    lax.fori_loop(0, field_ref.shape[0] // STRIP, strip, 0)


def send_rows(copies, field_ref, before_ref, after_ref):
    return [copies.launch(field_ref, before_ref, beside(1)), copies.launch(field_ref, after_ref, beside(-1))]


RITZ_LAYOUT = (128, [("core", "scatter"), ("z", "scatter"), ("x", "exchange"), ("y", "exchange")])
GRAM_LAYOUTS = [
    (768, [("core", "scatter"), ("x", "scatter"), ("y", "scatter"), ("z", "exchange")]),
    (512, [("core", "scatter"), ("y", "scatter"), ("x", "scatter"), ("z", "exchange")]),
    RITZ_LAYOUT,
]
GRAM_ROWS = 1408
AXES = ("core", "x", "y", "z")
COLUMNS = range(1, 8)


def fill_weights(own_ref, before_ref, rate, weight_ref):
    width = own_ref.shape[1]
    lane = lax.broadcasted_iota(jnp.int32, (1, width), 1)
    z, x = lane // NX, lane % NX
    place = lax.axis_index("vox") * 8 + lax.axis_index("col")
    first, last = place == 0, place == 255

    def shifted(value, distance):
        distance = distance % width
        return pltpu.roll(value, distance, axis=1) if distance else value

    def within(dz, dx):
        return (z + dz >= 0) & (z + dz < NZ) & (x + dx >= 0) & (x + dx < NX)

    table = {}
    for which, (dy, dz, dx) in enumerate(offsets):
        ahead = jnp.where(within(dz, dx), own_ref[which:which + 1, :], 0.0)
        source = before_ref if dy else own_ref
        back = jnp.where(within(-dz, -dx), shifted(source[which:which + 1, :], dz * NX + dx), 0.0)
        if dy:
            ahead = ahead * jnp.where(last, 0.0, 1.0)
            back = back * jnp.where(first, 0.0, 1.0)
        table[dy, dz, dx] = ahead
        table[-dy, -dz, -dx] = back
    degree = sum(table.values())
    k = 0
    for dx in (-1, 0, 1):
        for dy in (-1, 0, 1):
            same = degree + rate if (dy, dx) == (0, 0) else -table[dy, 0, dx]
            other = -(table[dy, 1, dx] + table[dy, -1, dx])
            for value in (same, other):
                weight_ref[k:k + 1, :] = shifted(value, dx)
                k += 1


def send_columns(copies, group_ref, row_ref):
    me = lax.axis_index("col")
    count, width = group_ref.shape[0], row_ref.shape[1]
    mine = pl.ds(pl.multiple_of(me * count, 8), count)
    sent = []
    for step in COLUMNS:
        voxels = pl.ds(pl.multiple_of(lax.rem(me + step, 8) * width, 128), width)
        sent.append(copies.launch(group_ref.at[:, voxels], row_ref.at[mine], column(step)))
    row_ref[mine, :] = group_ref[:, pl.ds(pl.multiple_of(me * width, 128), width)]
    return sent


def start_kernel(group_ref, dir_group_ref, coupling_ref, class_ref, relaxivity_ref,
                 modes_ref, dirs_ref, image_ref, dir_image_ref, weight_ref, damping_ref, ritz_ref, *scratch):
    before, after, dir_before, dir_after, coupling_before, local = scratch[:6]
    copies = Copies(*scratch[-2:])
    near = [beside(1), beside(-1)] + [column(step) for step in COLUMNS] + along(("y", "z"))
    near += along(("core", "x"))
    hail(near)
    rate = jnp.zeros(class_ref.shape, jnp.float32)
    for k in range(relaxivity_ref.shape[1]):
        rate = rate + jnp.where(class_ref[...] == k, relaxivity_ref[:, k:k + 1], 0.0)
    damping_ref[...] = 1.0 / (1.0 + rate)
    heard(near)
    coupled = copies.launch(coupling_ref, coupling_before, beside(1))
    arriving = send_columns(copies, group_ref, modes_ref)
    coupled.wait_recv()
    fill_weights(coupling_ref, coupling_before, rate, weight_ref)
    for copy in arriving:
        copy.wait_recv()
    halo = send_rows(copies, modes_ref, before, after)
    arriving = send_columns(copies, dir_group_ref, dirs_ref)
    for copy in halo:
        copy.wait_recv()
    apply_operator(modes_ref, before, after, weight_ref, image_ref)
    local[...] = product(modes_ref[...], image_ref[...], (1, 1))
    share = Share(RITZ_LAYOUT, 0, local, ritz_ref, scratch[6:-2], copies)
    share.begin()
    for copy in arriving:
        copy.wait_recv()
    halo = send_rows(copies, dirs_ref, dir_before, dir_after)
    share.turn()
    share.turn()
    for copy in halo:
        copy.wait_recv()
    apply_operator(dirs_ref, dir_before, dir_after, weight_ref, dir_image_ref)
    through([share])
    copies.drain()


def search_kernel(modes_ref, images_ref, dirs_ref, dir_images_ref, ritz_ref, damping_ref, weight_ref,
                  search_ref, search_image_ref, sum_ref, *scratch):
    n = 128
    before, after, local = scratch[:3]
    rest = list(scratch[3:-2])
    copies = Copies(*scratch[-2:])
    near = [beside(1), beside(-1)] + along(AXES)
    hail(near)
    search_ref[...] = (images_ref[...] - product(ritz_ref[...], modes_ref[...])) * damping_ref[...]
    heard(near)
    halo = send_rows(copies, search_ref, before, after)
    shares, start = [], 0
    for layout in GRAM_LAYOUTS:
        used = 2 * len(layout[1])
        shares.append(Share(layout, start, local, sum_ref, rest[:used], copies))
        rest, start = rest[used:], start + layout[0]

    def between(left_ref, right_ref):
        return product(left_ref[...], right_ref[...], (1, 1))

    def put(k, value):
        local[n * k:n * (k + 1)] = value

    row = lax.broadcasted_iota(jnp.int32, (n, n), 0)
    col = lax.broadcasted_iota(jnp.int32, (n, n), 1)
    put(0, between(search_ref, modes_ref))
    put(1, between(dirs_ref, modes_ref))
    put(2, between(dirs_ref, search_ref))
    put(3, between(search_ref, images_ref))
    put(4, between(dirs_ref, images_ref))
    put(5, between(dir_images_ref, search_ref))
    shares[0].begin()
    ends = jnp.zeros((n, n), jnp.float32)
    for k, (field_ref, field_image_ref) in enumerate(((modes_ref, images_ref), (dirs_ref, dir_images_ref))):
        field = between(field_ref, field_ref)
        put(6 + k, jnp.where(row >= col, between(field_ref, field_image_ref), field))
        ends = jnp.where(row == k, jnp.sum(jnp.where(row == col, field, 0.0), axis=0, keepdims=True), ends)
    put(8, between(search_ref, search_ref))
    put(9, ends)
    shares[1].begin()
    shares[0].turn()
    for copy in halo:
        copy.wait_recv()
    apply_operator(search_ref, before, after, weight_ref, search_image_ref)
    put(10, between(search_ref, search_image_ref))
    shares[2].begin()
    shares[1].turn()
    through(shares)
    copies.drain()


def finish_kernel(coeff_ref, modes_ref, search_ref, dirs_ref, group_ref, *scratch):
    n = 128
    copies = Copies(*scratch[-2:])
    final = scratch[0]
    near = [column(step) for step in COLUMNS]
    hail(near)
    total = product(coeff_ref[0:n], modes_ref[...], (0, 0)) + product(coeff_ref[n:2 * n], search_ref[...], (0, 0))
    final[...] = (total + product(coeff_ref[2 * n:], dirs_ref[...], (0, 0))) * math.sqrt(256 * final.shape[1])
    heard(near)
    me = lax.axis_index("col")
    count, width = group_ref.shape[0], final.shape[1]
    voxels = pl.ds(pl.multiple_of(me * width, 128), width)
    arriving = []
    for step in COLUMNS:
        other = pl.ds(pl.multiple_of(lax.rem(me + step, 8) * count, 8), count)
        arriving.append(copies.launch(final.at[other], group_ref.at[:, voxels], column(step)))
    group_ref[:, voxels] = final[pl.ds(pl.multiple_of(me * count, 8), count), :]
    for copy in arriving:
        copy.wait_recv()
    copies.drain()


def call_remote(kernel, name, collective_id, outs, scratch, layouts, operands, extra):
    scratch = [pltpu.VMEM(shape, jnp.float32) for shape in scratch]
    count = extra
    for layout in layouts:
        share_scratch, _, copies = plan(layout)
        scratch += share_scratch
        count += copies
    scratch += [pltpu.SemaphoreType.DMA((count,))] * 2
    vmem = pl.BlockSpec(memory_space=pltpu.VMEM)
    return pl.pallas_call(
        kernel,
        out_shape=tuple(jax.ShapeDtypeStruct(shape, jnp.float32) for shape in outs),
        in_specs=[vmem] * len(operands),
        out_specs=(vmem,) * len(outs),
        scratch_shapes=scratch,
        compiler_params=pltpu.CompilerParams(
            collective_id=collective_id, has_side_effects=True, vmem_limit_bytes=32 << 20
        ),
        name=name,
    )(*operands)


offsets = [
    (a, b, c) for a in (-1, 0, 1) for b in (-1, 0, 1) for c in (-1, 0, 1) if (a, b, c) > (0, 0, 0)
]


def matmul(left, right):
    return jnp.dot(left, right, precision=lax.Precision.HIGHEST, preferred_element_type=jnp.float32)


def symmetric(matrix):
    return 0.5 * (matrix + matrix.T)


def product(left, right, over=(1, 0)):
    return lax.dot_general(
        left, right, (((over[0],), (over[1],)), ((), ())),
        precision=lax.Precision.HIGHEST, preferred_element_type=jnp.float32,
    )


SETTLED = 2e-3
MOST_STEPS = 10


def inverse_factor(matrix, step_ref, work_ref):
    n = matrix.shape[0]
    row = lax.broadcasted_iota(jnp.int32, (n, n), 0)
    col = lax.broadcasted_iota(jnp.int32, (n, n), 1)
    same = row == col
    unit = jnp.where(same, 1.0, 0.0)
    diag = jnp.where(same, matrix, 0.0)
    scale_row = lax.rsqrt(jnp.sum(diag, axis=0, keepdims=True))
    scale_col = lax.rsqrt(jnp.sum(diag, axis=1, keepdims=True))
    scaled = scale_col * matrix * scale_row

    def half(error):
        return jnp.where(row > col, error, jnp.where(same, 0.5 * error, 0.0))

    start = scaled - unit
    step_ref[...] = unit - half(start)

    def going(carry):
        count, size = carry
        return jnp.logical_and(count < MOST_STEPS, jnp.logical_not(size < SETTLED * SETTLED))

    def step(carry):
        count, _ = carry
        now = step_ref[...]
        error = product(product(now, scaled), now, (1, 1)) - unit
        step_ref[...] = now - product(half(error), now)
        return count + 1, jnp.sum(error * error)

    _, size = lax.while_loop(going, step, (jnp.int32(0), jnp.sum(start * start)))

    @pl.when(jnp.logical_not(size < SETTLED * SETTLED))
    def _():
        work_ref[...] = scaled
        step_ref[...] = unit

        def eliminate(j, carry):
            work, done = work_ref[...], step_ref[...]
            pivot_row = jnp.sum(jnp.where(row == j, work, 0.0), axis=0, keepdims=True)
            pivot_col = jnp.sum(jnp.where(col == j, work, 0.0), axis=1, keepdims=True)
            done_row = jnp.sum(jnp.where(row == j, done, 0.0), axis=0, keepdims=True)
            pivot = jnp.sum(jnp.where(same & (row == j), work, 0.0))
            factor = jnp.where(row > j, pivot_col / pivot, 0.0)
            work_ref[...] = work - factor * pivot_row
            done = done - factor * done_row
            step_ref[...] = jnp.where(row == j, done * lax.rsqrt(jnp.full((1, n), pivot)), done)
            return carry

        lax.fori_loop(0, n, eliminate, 0)

    return step_ref[...] * scale_row


def pencil_kernel(sum_ref, coeff_ref, ritz_ref, image_ref, inverse_ref, step_ref, work_ref):
    n = 128

    def block(k):
        return sum_ref[n * k:n * (k + 1)]

    row = lax.broadcasted_iota(jnp.int32, (n, n), 0)
    col = lax.broadcasted_iota(jnp.int32, (n, n), 1)
    same = row == col
    def mirrored(lower):
        return jnp.where(row >= col, lower, lower.T)

    ends = sum_ref[9 * n:9 * n + 8]
    searched = block(10)
    images = [mirrored(block(6)), 0.5 * (searched + searched.T), mirrored(block(7))]
    fields = [mirrored(block(6).T), mirrored(block(8)), mirrored(block(7).T)]
    fields[0] = jnp.where(same, ends[0:1], fields[0])
    fields[2] = jnp.where(same, ends[1:2], fields[2])
    across, down, normed = [], [], {}
    for field in fields:
        diag = jnp.where(same, field, 0.0)
        across.append(lax.rsqrt(jnp.sum(diag, axis=0, keepdims=True) + 1e-06))
        down.append(lax.rsqrt(jnp.sum(diag, axis=1, keepdims=True) + 1e-06))
    for i in range(3):
        image_ref[n * i:n * (i + 1), n * i:n * (i + 1)] = images[i]
        normed[i, i] = down[i] * fields[i] * across[i]
    for k, (i, j) in enumerate(((1, 0), (2, 0), (2, 1))):
        image = block(3 + k)
        image_ref[n * i:n * (i + 1), n * j:n * (j + 1)] = image
        image_ref[n * j:n * (j + 1), n * i:n * (i + 1)] = image.T
        normed[i, j] = down[i] * block(k) * across[j]

    inverse_0 = inverse_factor(normed[0, 0], step_ref, work_ref)
    lower_10 = product(normed[1, 0], inverse_0, (1, 1))
    lower_20 = product(normed[2, 0], inverse_0, (1, 1))
    inverse_1 = inverse_factor(normed[1, 1] - product(lower_10, lower_10, (1, 1)), step_ref, work_ref)
    lower_21 = product(normed[2, 1] - product(lower_20, lower_10, (1, 1)), inverse_1, (1, 1))
    rest = normed[2, 2] - product(lower_20, lower_20, (1, 1)) - product(lower_21, lower_21, (1, 1))
    inverse_10 = -product(inverse_1, product(lower_10, inverse_0))
    inner_20 = product(lower_20, inverse_0) + product(lower_21, inverse_10)
    inner_21 = product(lower_21, inverse_1)
    inverse_2 = inverse_factor(rest, step_ref, work_ref)
    inverse_ref[...] = jnp.zeros((3 * n, 3 * n), jnp.float32)
    inverse_ref[0:n, 0:n] = inverse_0 * across[0]
    inverse_ref[n:2 * n, 0:n] = inverse_10 * across[0]
    inverse_ref[n:2 * n, n:2 * n] = inverse_1 * across[1]
    inverse_ref[2 * n:, 0:n] = -product(inverse_2, inner_20) * across[0]
    inverse_ref[2 * n:, n:2 * n] = -product(inverse_2, inner_21) * across[1]
    inverse_ref[2 * n:, 2 * n:] = inverse_2 * across[2]
    reduced = product(product(inverse_ref[...], image_ref[...]), inverse_ref[...], (1, 1))
    shift = 2.0 * jnp.max(jnp.sum(jnp.abs(reduced), axis=1, keepdims=True))
    reduced = reduced * (1.0 / jnp.full((1, 3 * n), shift))
    tall_row = lax.broadcasted_iota(jnp.int32, (3 * n, n), 0)
    tall_col = lax.broadcasted_iota(jnp.int32, (3 * n, n), 1)
    iterate = jnp.where(tall_row == tall_col, 1.0, 0.0) - reduced[:, :n]
    for _ in range(QSTEPS - 1):
        iterate = iterate - product(reduced, iterate)
    factor = inverse_factor(product(iterate, iterate, (0, 0)), step_ref, work_ref)
    iterate = product(iterate, factor, (1, 1))
    coeffs = product(inverse_ref[...], iterate, (0, 0))
    coeff_ref[...] = coeffs
    quotient = product(coeffs, product(image_ref[...], coeffs), (0, 0))
    ritz_ref[...] = 0.5 * (quotient + quotient.T)


def solve_pencil(summed):
    n = 128
    square = pltpu.VMEM((3 * n, 3 * n), jnp.float32)
    small = pltpu.VMEM((n, n), jnp.float32)
    return pl.pallas_call(
        pencil_kernel,
        out_shape=(jax.ShapeDtypeStruct((3 * n, n), jnp.float32), jax.ShapeDtypeStruct((n, n), jnp.float32)),
        in_specs=[pl.BlockSpec(memory_space=pltpu.VMEM)],
        out_specs=[pl.BlockSpec(memory_space=pltpu.VMEM)] * 2,
        scratch_shapes=[square, square, small, small],
        compiler_params=pltpu.CompilerParams(vmem_limit_bytes=32 << 20),
        name="pencil",
    )(summed)


def on_device(start_modes, start_dirs, coupling, relax_class, relaxivity):
    local_voxels = coupling.shape[1]
    count = start_modes.shape[0] * 8
    row, line, small = (count, local_voxels), (1, local_voxels), (count, count)
    modes, dirs, images, dir_images, weights, damping, ritz = call_remote(
        start_kernel, "start", 1, (row, row, row, row, (18, local_voxels), line, small),
        [row, row, row, row, coupling.shape, small], [RITZ_LAYOUT],
        (start_modes, start_dirs, coupling, relax_class[None, :], relaxivity[None, :]), 19,
    )
    ritz = symmetric(ritz)
    for iteration in range(ITERS):
        search, search_images, summed = call_remote(
            search_kernel, "search", 2, (row, row, (GRAM_ROWS, count)), [row, row, (GRAM_ROWS, count)], GRAM_LAYOUTS,
            (modes, images, dirs, dir_images, ritz, damping, weights), 2,
        )
        coeffs, ritz = solve_pencil(summed)
        if iteration < ITERS - 1:
            basis = jnp.concatenate([modes, search, dirs], axis=0)
            basis_images = jnp.concatenate([images, search_images, dir_images], axis=0)
            modes = matmul(coeffs.T, basis)
            images = matmul(coeffs.T, basis_images)
            dirs = matmul(coeffs[count:].T, basis[count:])
            dir_images = matmul(coeffs[count:].T, basis_images[count:])
    modes_out, = call_remote(
        finish_kernel, "finish", 3, (start_modes.shape,), [row], [], (coeffs, modes, search, dirs), 7
    )
    return (modes_out, ritz)


def solution(mesh):
    in_specs = (P("col", "vox"), P("col", "vox"), P(None, ("vox", "col")), P(("vox", "col")), P())
    out_specs = (P("col", "vox"), P())
    return jax.shard_map(
        on_device, mesh=mesh, in_specs=in_specs, out_specs=out_specs, check_vma=False
    )
```
